256 devices in a mesh: pipe: 16 (over y, z_hi), ep: 16 (over z_lo, x, core).
Axes of the slice: x: 4, y: 4, z: 8 (z_hi: 4, z_lo: 2; z = z_hi * 2 + z_lo), core: 2. Of those that a mesh axis runs over, the one named last changes fastest.
Arguments:
- forward_states: bfloat16 [16, 1024, 7168], P('pipe', 'ep'), may hold values from -6 to 6
- reverse_states: bfloat16 [16, 1024, 7168], P('pipe', 'ep'), may hold values from -6 to 6
- forward_routes: int32 [1, 16, 1024, 1], P(None, 'pipe'), may hold values from 0 to 1; in each aligned block of 64 rows (0 to 63, 64 to 127, ..., all dimensions but the last counted through in order) at most 32 rows name the same one
- reverse_routes: int32 [1, 16, 1024, 1], P(None, 'pipe'), may hold values from 0 to 1; in each aligned block of 64 rows (0 to 63, 64 to 127, ..., all dimensions but the last counted through in order) at most 32 rows name the same one
- forward_share: float32 [1, 16, 1024], P(None, 'pipe', 'ep'), may hold values from 0.2 to 2.5
- reverse_share: float32 [1, 16, 1024], P(None, 'pipe', 'ep'), may hold values from 0.2 to 2.5
- layer_gate: bfloat16 [16, 7168, 2048], P('pipe', None, 'ep'), may hold values from -0.0625 to 0.0625
- layer_up: bfloat16 [16, 7168, 2048], P('pipe', None, 'ep'), may hold values from -0.0625 to 0.0625
- layer_down: bfloat16 [16, 2048, 7168], P('pipe', 'ep'), may hold values from -0.1875 to 0.1875
Outputs:
- forward_out: bfloat16 [16, 1024, 7168], P('pipe', 'ep')
- reverse_out: bfloat16 [16, 1024, 7168], P('pipe', 'ep')
The draws below stay inside these ranges and needn't reach their ends.
Inputs may be any that keep to these rules, and one draw needn't show every extreme that they name: `forward_routes`: in each step, section and aligned block of 64 tokens (the tokens of one device), exactly 32 tokens name each expert. `reverse_routes`: in each step, section and aligned block of 64 tokens (the tokens of one device), exactly 32 tokens name each expert.
All inputs are finite; a program needn't handle non-finite values.
Results may differ from the reference program's by a relative error of at most 0.0052.
Values may be sent and summed in bfloat16 or wider, within the bound.
No kernel may reach another device: no remote copies, remote signals or barrier semaphores. Data moves between devices by JAX's collectives and lax.ppermute only.
A program may use at most 128 MiB of HBM per device.

```python
import math
import jax
import jax.numpy as jnp
import numpy as np
from jax import lax

D = 7168
FF = 1024
EXPERTS = 2
TICKS = 1
TOK_DEV = 64
SECTIONS = 16
TOKENS = 1024
N_EP = 16


def block_scale(stream_key, shape, pieces, smallest, largest):
    gain = 1.0
    for axis_at, blocks in pieces:
        heights = jax.random.uniform(jax.random.fold_in(jax.random.fold_in(stream_key, 6), axis_at), (blocks,), jnp.float32, smallest / len(pieces), largest / len(pieces))
        gain = gain * jnp.repeat(jnp.exp(heights), shape[axis_at] // blocks).reshape((-1,) + (1,) * (len(shape) - 1 - axis_at))
    return gain


def shared_out(key, own, number, rows, count, top, reach, slope):
    sequence = jax.random.permutation(key, count)
    packed, ordinary = portions_of(count, rows * top, reach, slope, True), portions_of(count, rows * top, reach, slope, False)
    places = jnp.arange(count)

    def named(tallies, offset_by):
        used = int((tallies > 0).sum())
        fixed = max(1, used // 4)
        shifted = fixed + (places - fixed + offset_by * (used - fixed)) % max(1, count - fixed)
        return jnp.zeros((count,), jnp.int32).at[sequence[jnp.where(places < fixed, places, shifted)]].set(jnp.asarray(tallies, jnp.int32))

    tallies = jnp.where(number % 4 == 0, named(packed, number // 4), named(ordinary, number - number // 4 - 1))
    mixed = jax.random.permutation(jax.random.fold_in(own, 3), count)
    giver, sink = mixed[0:count // 2 * 2:2], mixed[1:count // 2 * 2:2]
    slack = jnp.minimum(tallies[giver] - 1, reach - tallies[sink]) // 2
    slack = jnp.where((giver == sequence[0]) | (sink == sequence[0]) | (tallies[sink] == 0), 0, jnp.maximum(slack, 0))
    shifted = jax.random.randint(jax.random.fold_in(own, 4), (count // 2,), 0, 1 << 20) % (slack + 1)
    tallies = tallies.at[giver].add(-shifted).at[sink].add(shifted)
    members = jnp.searchsorted(jnp.cumsum(tallies), jnp.arange(rows * top), side="right").astype(jnp.int32)
    grid = members.reshape(top, rows).T
    grid = grid[jax.random.permutation(jax.random.fold_in(own, 1), rows)]
    offset_by = jax.random.randint(jax.random.fold_in(own, 2), (rows, 1), 0, top)
    return jnp.take_along_axis(grid, (jnp.arange(top)[None, :] + offset_by) % top, axis=1)


def portions_of(number_of, total, reach, lean, full):
    weights = [(1 << 20) // math.isqrt(rank ** lean) + 1 for rank in range(1, number_of + 1)]
    largest = reach if full else min(reach, max(-(-total // number_of), total * weights[0] // sum(weights)))
    least = 1 if total - largest >= number_of - 1 else 0
    counts, spare = [largest] + [least] * (number_of - 1), total - largest - least * (number_of - 1)
    while spare > 0:
        movable = [i for i in range(1, number_of) if counts[i] < largest] or [i for i in range(1, number_of) if counts[i] < reach]
        pool, budget = sum([weights[i] for i in movable]), spare
        for i in movable:
            extra = min(reach - counts[i], max(1, budget * weights[i] // pool), spare)
            counts[i] = counts[i] + extra
            spare = spare - extra
    return np.array(counts)


def bell_draw(stream_key, extent, deviation, limit, cuts=(), held_as=jnp.bfloat16):
    loudness = block_scale(stream_key, extent, cuts, -0.22, 0.18) if cuts else 1.0
    drawn = jax.random.normal(stream_key, extent, jnp.float32) * deviation * loudness
    return jnp.minimum(jnp.maximum(drawn, -limit), limit).astype(held_as)


def setup_inputs(seed: int = 0) -> dict:
    key_of = jax.random.split(jax.random.key(seed), 10)
    forward_states = bell_draw(key_of[0], (SECTIONS, TOKENS, D), 1.0, 6.0, ((0, 16), (1, 16)))
    reverse_states = bell_draw(key_of[1], (SECTIONS, TOKENS, D), 1.0, 6.0, ((0, 16), (1, 16)))
    forward_routes_keys = jax.random.split(jax.random.fold_in(key_of[2], 1), TICKS * SECTIONS * TOKENS // TOK_DEV)
    forward_routes_turns = jax.random.permutation(jax.random.fold_in(key_of[2], 3), TICKS * SECTIONS * TOKENS // TOK_DEV)
    forward_routes = jax.vmap(lambda own, number: shared_out(jax.random.fold_in(key_of[2], 2), own, number, TOK_DEV, EXPERTS, 1, TOK_DEV // EXPERTS, 0))(forward_routes_keys, forward_routes_turns).reshape((TICKS, SECTIONS, TOKENS, 1))
    reverse_routes_keys = jax.random.split(jax.random.fold_in(key_of[3], 1), TICKS * SECTIONS * TOKENS // TOK_DEV)
    reverse_routes_turns = jax.random.permutation(jax.random.fold_in(key_of[3], 3), TICKS * SECTIONS * TOKENS // TOK_DEV)
    reverse_routes = jax.vmap(lambda own, number: shared_out(jax.random.fold_in(key_of[3], 2), own, number, TOK_DEV, EXPERTS, 1, TOK_DEV // EXPERTS, 0))(reverse_routes_keys, reverse_routes_turns).reshape((TICKS, SECTIONS, TOKENS, 1))
    forward_share = jnp.clip(0.2 + 2.3 * jax.random.uniform(key_of[4], (TICKS, SECTIONS, TOKENS), jnp.float32) ** block_scale(key_of[4], (TICKS, SECTIONS, TOKENS), ((1, 16), (2, 16)), -0.2, 0.2), 0.2, 2.5)
    reverse_share = jnp.clip(0.2 + 2.3 * jax.random.uniform(key_of[5], (TICKS, SECTIONS, TOKENS), jnp.float32) ** block_scale(key_of[5], (TICKS, SECTIONS, TOKENS), ((1, 16), (2, 16)), -0.2, 0.2), 0.2, 2.5)
    layer_gate = bell_draw(key_of[6], (SECTIONS, D, EXPERTS * FF), D ** -0.5, 0.0625, ((0, 16), (2, 16)))
    layer_up = bell_draw(key_of[7], (SECTIONS, D, EXPERTS * FF), D ** -0.5, 0.0625, ((0, 16), (2, 16)))
    layer_down = bell_draw(key_of[8], (SECTIONS, EXPERTS * FF, D), FF ** -0.5, 0.1875, ((0, 16), (1, 16)))
    return {"forward_states": forward_states, "reverse_states": reverse_states, "forward_routes": forward_routes, "reverse_routes": reverse_routes, "forward_share": forward_share, "reverse_share": reverse_share, "layer_gate": layer_gate, "layer_up": layer_up, "layer_down": layer_down}


def layer(states, routes, share, gate, up, down):
    slices = N_EP // EXPERTS
    width = FF // slices
    order = jnp.argsort(routes, stable=True).astype(jnp.int32).reshape(EXPERTS, TOKENS // EXPERTS)
    branch = jnp.zeros((TOKENS, D), jnp.float32)
    for expert in range(EXPERTS):
        picked = order[expert]
        rows = states[picked]
        gated = jnp.dot(rows, gate[:, expert * FF:(expert + 1) * FF], preferred_element_type=jnp.float32)
        upward = jnp.dot(rows, up[:, expert * FF:(expert + 1) * FF], preferred_element_type=jnp.float32)
        hidden = (jax.nn.silu(gated) * upward).astype(jnp.bfloat16)
        lower = down[expert * FF:(expert + 1) * FF].reshape(slices, width, D).astype(jnp.float32)
        parts = jnp.einsum("nsh,shd->snd", hidden.reshape(-1, slices, width).astype(jnp.float32), lower)
        parts = lax.optimization_barrier(parts.astype(jnp.bfloat16)).astype(jnp.float32)
        branch = branch.at[picked].set(jnp.sum(parts, axis=0))
    return (states.astype(jnp.float32) + share[:, None] * branch).astype(jnp.bfloat16)


def section_map(states, routes, share, gate, up, down):
    def single(items):
        return layer(*items)
    return lax.map(single, (states, routes, share, gate, up, down))


def reference(forward_states, reverse_states, forward_routes, reverse_routes, forward_share, reverse_share, layer_gate, layer_up, layer_down):
    ahead = forward_states
    behind = reverse_states
    for tick in range(TICKS):
        ahead = section_map(ahead, forward_routes[tick, :, :, 0], forward_share[tick], layer_gate, layer_up, layer_down)
        behind = section_map(behind, reverse_routes[tick, :, :, 0], reverse_share[tick], layer_gate, layer_up, layer_down)
        ahead = jnp.concatenate([jnp.zeros_like(ahead[:1]), ahead[:-1]], axis=0)
        behind = jnp.concatenate([behind[1:], jnp.zeros_like(behind[:1])], axis=0)
    return ahead, behind
```

```python
import functools

import jax
import jax.numpy as jnp
from jax import lax
from jax.experimental import pallas as pl
from jax.experimental.pallas import tpu as pltpu
from jax.sharding import PartitionSpec as P

EXPERTS = 2
RING = 4
CORES = 2
OFFSETS = (0, -1, 1, 2)
PLACE = {offset % RING: at for at, offset in enumerate(OFFSETS)}
VMEM_LIMIT = 16 * 1024 * 1024


def move(shard, pipes, by=0, flip=False, steps=0, core=False):
    pairs = []
    for pipe in range(pipes):
        if not 0 <= pipe + by < pipes:
            continue
        for z in range(EXPERTS):
            for x in range(RING):
                for c in range(CORES):
                    source = ((pipe * EXPERTS + z) * RING + x) * CORES + c
                    z_to = 1 - z if flip else z
                    x_to = (x + steps) % RING
                    c_to = 1 - c if core else c
                    pairs.append(
                        (source, (((pipe + by) * EXPERTS + z_to) * RING + x_to) * CORES + c_to)
                    )
    return lax.ppermute(shard, ("pipe", "ep"), pairs)


def picks(routes, expert, capacity):
    count = routes.shape[1]
    match = (routes == expert).astype(jnp.float32)
    upto = (
        lax.broadcasted_iota(jnp.int32, (count, count), 0)
        <= lax.broadcasted_iota(jnp.int32, (count, count), 1)
    ).astype(jnp.float32)
    rank = jnp.dot(match, upto, preferred_element_type=jnp.float32)
    slots = lax.broadcasted_iota(jnp.int32, (capacity, count), 0).astype(jnp.float32) + 1.0
    return jnp.where((rank == slots) & (match > 0.0), 1.0, 0.0)


def slices_kernel(x_ref, down, *refs):
    outs, sems = refs[:-1], refs[-1]
    columns = outs[0].shape[1]
    copies = []
    for at, (offset, out) in enumerate(zip(OFFSETS, outs)):
        start = pl.multiple_of(lax.rem(x_ref[0] - offset + RING, RING) * columns, 128)
        copies.append(
            pltpu.make_async_copy(down.at[:, pl.ds(start, columns)], out, sems.at[at])
        )
    for copy in copies:
        copy.start()
    for copy in copies:
        copy.wait()


def slices(x, down):
    depth, width = down.shape
    return pl.pallas_call(
        slices_kernel,
        in_specs=[
            pl.BlockSpec(memory_space=pltpu.SMEM),
            pl.BlockSpec(memory_space=pltpu.HBM),
        ],
        out_specs=[pl.BlockSpec(memory_space=pltpu.VMEM)] * RING,
        out_shape=[jax.ShapeDtypeStruct((depth, width // RING), down.dtype)] * RING,
        scratch_shapes=[pltpu.SemaphoreType.DMA((RING,))],
        compiler_params=pltpu.CompilerParams(vmem_limit_bytes=VMEM_LIMIT),
        name="slices",
    )(x, pltpu.with_memory_space_constraint(down, pltpu.HBM))


def pack_kernel(place, fr, rr, fs, rs, fx, rx, *refs):
    (own_f, own_r, oth, fr_v, rr_v, fs_v, rs_v, fx_v, rx_v, sems) = refs
    count, width = fx.shape
    capacity = count // EXPERTS
    copies = [
        pltpu.make_async_copy(source, target, sems.at[at])
        for at, (source, target) in enumerate(
            ((fr, fr_v), (rr, rr_v), (fs, fs_v), (rs, rs_v), (fx, fx_v), (rx, rx_v))
        )
    ]
    for copy in copies:
        copy.start()
    mine, z = place[0], place[1]
    every = fr.shape[1]
    lane = lax.broadcasted_iota(jnp.int32, (capacity, 128), 1)
    token = lax.broadcasted_iota(jnp.int32, (capacity, count), 1).astype(jnp.float32)
    local = (
        lax.broadcasted_iota(jnp.int32, (every, count), 0)
        == lax.broadcasted_iota(jnp.int32, (every, count), 1) + mine * count
    ).astype(jnp.bfloat16)
    for copy in copies[:4]:
        copy.wait()
    found = []
    for routes, share in ((fr_v, fs_v), (rr_v, rs_v)):
        routes = jnp.dot(
            routes[...].astype(jnp.bfloat16), local, preferred_element_type=jnp.float32
        )
        routes = (routes > 0.5).astype(jnp.int32)
        for expert in (z, 1 - z):
            pick = picks(routes, expert, capacity)
            rest = jnp.sum(pick * share[...], axis=1, keepdims=True)
            tail = jnp.where(lane == 3, jnp.sum(pick * token, axis=1, keepdims=True), 0.0)
            for at_term in range(3):
                term = rest.astype(jnp.bfloat16).astype(jnp.float32)
                tail = jnp.where(lane == at_term, term, tail)
                rest = rest - term
            found.append((pick.astype(jnp.bfloat16), tail.astype(jnp.bfloat16)))
    for at, rows in enumerate((fx_v, rx_v)):
        copies[4 + at].wait()
        for side in range(2):
            pick, tail = found[2 * at + side]
            out = oth if side else (own_f, own_r)[at]
            part = slice(at * capacity, (at + 1) * capacity) if side else slice(None)
            out[part, :width] = jnp.dot(
                pick, rows[...], preferred_element_type=jnp.float32
            ).astype(jnp.bfloat16)
            out[part, width:] = tail


def pack(place, *arrays):
    count, width = arrays[4].shape
    every = arrays[0].shape[1]
    return pl.pallas_call(
        pack_kernel,
        in_specs=[pl.BlockSpec(memory_space=pltpu.SMEM)]
        + [pl.BlockSpec(memory_space=pltpu.HBM)] * 6,
        out_specs=[pl.BlockSpec(memory_space=pltpu.VMEM)] * 3,
        out_shape=[
            jax.ShapeDtypeStruct((rows, width + 128), jnp.bfloat16)
            for rows in (count // 2, count // 2, count)
        ],
        scratch_shapes=[pltpu.VMEM((1, every), jnp.int32)] * 2
        + [pltpu.VMEM((1, count), jnp.float32)] * 2
        + [pltpu.VMEM((count, width), jnp.bfloat16)] * 2
        + [pltpu.SemaphoreType.DMA((6,))],
        compiler_params=pltpu.CompilerParams(vmem_limit_bytes=VMEM_LIMIT),
        name="pack",
    )(place, *[pltpu.with_memory_space_constraint(a, pltpu.HBM) for a in arrays])


def hidden_kernel(steps, *refs):
    rows, (go, gt, uo, ut), (out, gated, upward) = refs[:-7], refs[-7:-3], refs[-3:]
    block = go.shape[0] // steps

    def step(at, _):
        part = pl.ds(pl.multiple_of(at * block, 128), block)
        x = jnp.concatenate([r[:, part] for r in rows], axis=0)
        g = jnp.concatenate([go[part, :], gt[part, :]], axis=1)
        u = jnp.concatenate([uo[part, :], ut[part, :]], axis=1)
        gated[...] += jnp.dot(x, g, preferred_element_type=jnp.float32)
        upward[...] += jnp.dot(x, u, preferred_element_type=jnp.float32)
        return 0

    gated[...] = jnp.zeros_like(gated)
    upward[...] = jnp.zeros_like(upward)
    lax.fori_loop(0, steps, step, 0, unroll=True)
    out[...] = (jax.nn.silu(gated[...]) * upward[...]).astype(jnp.bfloat16)


def hidden_rows(rows, weights):
    width, lanes = weights[0].shape
    count = sum(r.shape[0] for r in rows)
    whole = pl.BlockSpec(memory_space=pltpu.VMEM)
    return pl.pallas_call(
        functools.partial(hidden_kernel, 7),
        in_specs=[whole] * (len(rows) + 4),
        out_specs=whole,
        out_shape=jax.ShapeDtypeStruct((count, 2 * lanes), jnp.bfloat16),
        scratch_shapes=[pltpu.VMEM((count, 2 * lanes), jnp.float32)] * 2,
        compiler_params=pltpu.CompilerParams(vmem_limit_bytes=VMEM_LIMIT),
        cost_estimate=pl.CostEstimate(
            flops=8 * count * width * lanes,
            bytes_accessed=2 * width * (count + 4 * lanes),
            transcendentals=count * 2 * lanes,
        ),
        name="hidden",
    )(*rows, *weights)


def out_kernel(steps, x_ref, *refs):
    rows, hidden, down, outs, h = refs[:8], refs[8:12], refs[12:14], refs[14:18], refs[18]
    pair = 2 * rows[0].shape[0]
    lanes = hidden[0].shape[1] // 2
    columns = down[0].shape[1]
    width = RING * columns
    block = columns // steps
    for at, o in enumerate(OFFSETS):
        for core in range(CORES):
            for index, (s, source) in enumerate(zip(OFFSETS, hidden)):
                place = PLACE[(o - s) % RING]
                h[
                    at * pair : (at + 1) * pair,
                    (core * RING + index) * lanes : (core * RING + index + 1) * lanes,
                ] = source[place * pair : (place + 1) * pair, core * lanes : (core + 1) * lanes]
    terms = jnp.concatenate([r[:, width:] for r in rows], axis=0).astype(jnp.float32)
    share = terms[:, 0:1] + terms[:, 1:2] + terms[:, 2:3]

    def step(j, _):
        part = pl.ds(pl.multiple_of(j * block, 128), block)
        there = pl.ds(pl.multiple_of(x_ref[0] * columns + j * block, 128), block)
        d = jnp.concatenate([r[:, part] for r in down], axis=0)
        branch = jnp.dot(h[...], d, preferred_element_type=jnp.float32)
        states = jnp.concatenate([r[:, there] for r in rows], axis=0).astype(jnp.float32)
        result = (states + share * branch).astype(jnp.bfloat16)
        for at, out in enumerate(outs):
            out[:, part] = result[at * pair : (at + 1) * pair]
        return 0

    lax.fori_loop(0, steps, step, 0, unroll=True)


def out_rows(x, rows, hidden, down):
    half, wide = rows[0].shape
    pair = 2 * half
    count = RING * pair
    columns = (wide - 128) // RING
    lanes = hidden[0].shape[1]
    whole = pl.BlockSpec(memory_space=pltpu.VMEM)
    return pl.pallas_call(
        functools.partial(out_kernel, 7),
        in_specs=[pl.BlockSpec(memory_space=pltpu.SMEM)] + [whole] * 14,
        out_specs=[whole] * 4,
        out_shape=[jax.ShapeDtypeStruct((pair, columns), jnp.bfloat16)] * 4,
        scratch_shapes=[pltpu.VMEM((count, RING * lanes), jnp.bfloat16)],
        compiler_params=pltpu.CompilerParams(vmem_limit_bytes=VMEM_LIMIT),
        cost_estimate=pl.CostEstimate(
            flops=2 * count * columns * 4 * lanes,
            bytes_accessed=2 * columns * (2 * count + 4 * lanes),
            transcendentals=0,
        ),
        name="out",
    )(x, *rows, *hidden, *down)


def stack_kernel(*refs):
    depth = refs[0].shape[0]
    for at, piece in enumerate(refs[:-1]):
        refs[-1][at * depth : (at + 1) * depth, :] = piece[...]


def stack(pieces):
    depth, columns = pieces[0].shape
    block = columns // 2
    return pl.pallas_call(
        stack_kernel,
        grid=(2,),
        in_specs=[pl.BlockSpec((depth, block), lambda j: (0, j))] * 4,
        out_specs=pl.BlockSpec((4 * depth, block), lambda j: (0, j)),
        out_shape=jax.ShapeDtypeStruct((4 * depth, columns), jnp.bfloat16),
        compiler_params=pltpu.CompilerParams(vmem_limit_bytes=VMEM_LIMIT),
        name="stack",
    )(*pieces)


def regroup_kernel(x_ref, *refs):
    tails, pieces, outs = refs[:2], refs[2:6], refs[6:]
    pair, columns = pieces[0].shape
    capacity = pair // 2
    for direction, out in enumerate(outs):
        part = slice(direction * capacity, (direction + 1) * capacity)
        for offset, piece in zip(OFFSETS, pieces):
            start = pl.multiple_of(lax.rem(x_ref[0] - offset + RING, RING) * columns, 128)
            out[:, pl.ds(start, columns)] = piece[part, :]
        out[:, RING * columns :] = tails[direction][...]


def regroup(x, rows, pieces):
    pair, columns = pieces[0].shape
    wide = RING * columns + 128
    whole = pl.BlockSpec((pair, columns), lambda j, x: (0, 0))
    return pl.pallas_call(
        regroup_kernel,
        grid_spec=pltpu.PrefetchScalarGridSpec(
            num_scalar_prefetch=1,
            grid=(1,),
            in_specs=[pl.BlockSpec((pair // 2, 128), lambda j, x: (0, RING * columns // 128))] * 2
            + [whole] * 4,
            out_specs=[pl.BlockSpec((pair // 2, wide), lambda j, x: (0, 0))] * 2,
        ),
        out_shape=[jax.ShapeDtypeStruct((pair // 2, wide), jnp.bfloat16)] * 2,
        compiler_params=pltpu.CompilerParams(vmem_limit_bytes=VMEM_LIMIT),
        name="regroup",
    )(x, *rows, *pieces)


def merge_kernel(*refs):
    pieces, outs = refs[:-2], refs[-2:]
    count, width = outs[0].shape
    token = lax.broadcasted_iota(jnp.int32, (count, count), 1).astype(jnp.float32)
    for direction, out in enumerate(outs):
        mine = pieces[direction::2]
        rows = jnp.concatenate([piece[:, :width] for piece in mine], axis=0)
        place = jnp.concatenate([piece[:, width:] for piece in mine], axis=0).astype(jnp.float32)
        pick = jnp.where(place[:, 3:4] == token, 1.0, 0.0).astype(jnp.bfloat16)
        out[...] = lax.dot_general(
            pick, rows, (((0,), (0,)), ((), ())), preferred_element_type=jnp.float32
        ).astype(jnp.bfloat16)


def merge(pieces):
    count = sum(piece.shape[0] for piece in pieces) // 2
    whole = pl.BlockSpec(memory_space=pltpu.VMEM)
    shape = jax.ShapeDtypeStruct((count, pieces[0].shape[1] - 128), jnp.bfloat16)
    return pl.pallas_call(
        merge_kernel,
        in_specs=[whole] * len(pieces),
        out_specs=[whole] * 2,
        out_shape=[shape] * 2,
        compiler_params=pltpu.CompilerParams(vmem_limit_bytes=VMEM_LIMIT),
        name="merge",
    )(*pieces)


def after(values, deps):
    return lax.optimization_barrier((tuple(values), tuple(deps)))[0]


def per_device(
    forward_states,
    reverse_states,
    forward_routes,
    reverse_routes,
    forward_share,
    reverse_share,
    layer_gate,
    layer_up,
    layer_down,
):
    pipes = lax.axis_size("pipe")
    send = functools.partial(move, pipes=pipes)
    mine = lax.axis_index("ep").astype(jnp.int32)
    z = mine // (RING * CORES)
    x = (mine // CORES) % RING
    count, width = forward_states.shape[1:]
    columns = width // RING
    gate, up, down = layer_gate[0], layer_up[0], layer_down[0]

    at_x = x[None]

    def spread(h):
        return [h] + [send(h, steps=-o) for o in OFFSETS[1:]]

    def back(outs, flip):
        return [
            send(out, steps=o, flip=flip) if flip or o else out for out, o in zip(outs, OFFSETS)
        ]

    def first(f, r):
        return send(f, steps=1), send(r, steps=-1)

    def second(f, r):
        return send(r, steps=1), send(f, steps=-1)

    with jax.named_scope("weights"):
        weights = [gate, send(gate, core=True), up, send(up, core=True)]

    with jax.named_scope("pack"):
        own_f, own_r, oth = pack(
            jnp.stack([mine, z]),
            forward_routes.reshape(1, -1),
            reverse_routes.reshape(1, -1),
            forward_share.reshape(1, count),
            reverse_share.reshape(1, count),
            forward_states[0],
            reverse_states[0],
        )
    half = count // 2
    oth_f, oth_r = oth[:half], oth[half:]
    with jax.named_scope("swap"):
        swapped = send(oth, flip=True)
    with jax.named_scope("first1"):
        own_left_f, own_right_r = first(own_f, own_r)

    with jax.named_scope("down"):
        parts = list(slices(after((at_x,), (own_f,))[0], down))
        parts[1:3] = after(parts[1:3], (weights[1], weights[3]))
        parts[1:3] = [send(part, steps=-o) for part, o in zip(parts[1:3], OFFSETS[1:3])]

    with jax.named_scope("far1"):
        own_left_f, own_right_r, swapped, *_ = after(
            (own_left_f, own_right_r, swapped), parts[1:3]
        )
        far_f, far_r = first(own_left_f, own_right_r)
    with jax.named_scope("second1"):
        left_r, right_f = second(*after((own_f, own_r), (own_left_f, own_right_r)))
    rows1 = [own_f, own_r, own_left_f, left_r, right_f, own_right_r, far_f, far_r]
    with jax.named_scope("down"):
        parts[3:] = after(parts[3:], rows1)
        parts[3] = send(parts[3], steps=-OFFSETS[3])
    with jax.named_scope("hidden1"):
        hidden1 = spread(hidden_rows(rows1, weights))
    with jax.named_scope("down"):
        half_down = stack(after(parts, hidden1[:1]))
        down = [half_down, send(half_down, core=True)]
    with jax.named_scope("first0"):
        (swapped,) = after((swapped,), parts[3:] + hidden1[1:])
        f, r = swapped[:half], swapped[half:]
        left_f, right_r = first(f, r)
    with jax.named_scope("out1"):
        outs1 = out_rows(at_x, rows1, hidden1, down)
    with jax.named_scope("back1"):
        back1 = back(outs1, False)
    with jax.named_scope("far0"):
        far_f, far_r = first(*after((left_f, right_r), outs1))
    with jax.named_scope("second0"):
        left_r, right_f = second(*after((f, r), back1))
    rows0 = [f, r, left_f, left_r, right_f, right_r, far_f, far_r]
    with jax.named_scope("relay1"):
        whole_f, whole_r = regroup(at_x, (own_f, own_r), back1)
        sent1 = [send(whole_f, by=1), send(whole_r, by=-1)]
    with jax.named_scope("hidden0"):
        hidden0 = spread(hidden_rows(after(rows0, (whole_f, whole_r)), weights))
    with jax.named_scope("out0"):
        outs0 = out_rows(at_x, rows0, after(hidden0, sent1), down)
    with jax.named_scope("back0"):
        back0 = back(outs0, True)
    with jax.named_scope("relay0"):
        whole_f, whole_r = regroup(at_x, (oth_f, oth_r), back0)
        sent0 = [send(whole_f, by=1), send(whole_r, by=-1)]
    with jax.named_scope("merge"):
        ahead, behind = merge(sent1 + sent0)
    return (ahead[None], behind[None])


def solution(mesh):
    in_specs = (
        P("pipe", "ep", None),
        P("pipe", "ep", None),
        P(None, "pipe", None, None),
        P(None, "pipe", None, None),
        P(None, "pipe", "ep"),
        P(None, "pipe", "ep"),
        P("pipe", None, "ep"),
        P("pipe", None, "ep"),
        P("pipe", "ep", None),
    )
    out_specs = (P("pipe", "ep", None), P("pipe", "ep", None))
    return jax.shard_map(
        per_device, mesh=mesh, in_specs=in_specs, out_specs=out_specs, check_vma=False
    )
```

```python
import functools

import jax
import jax.numpy as jnp
from jax import lax
from jax.experimental import pallas as pl
from jax.experimental.pallas import tpu as pltpu
from jax.sharding import PartitionSpec as P

EXPERTS = 2
RING = 4
CORES = 2
OFFSETS = (0, -1, 1, 2)
PLACE = {offset % RING: at for at, offset in enumerate(OFFSETS)}
VMEM_LIMIT = 16 * 1024 * 1024


def move(shard, pipes, by=0, flip=False, steps=0, core=False):
    pairs = []
    for pipe in range(pipes):
        if not 0 <= pipe + by < pipes:
            continue
        for z in range(EXPERTS):
            for x in range(RING):
                for c in range(CORES):
                    source = ((pipe * EXPERTS + z) * RING + x) * CORES + c
                    z_to = 1 - z if flip else z
                    x_to = (x + steps) % RING
                    c_to = 1 - c if core else c
                    pairs.append(
                        (source, (((pipe + by) * EXPERTS + z_to) * RING + x_to) * CORES + c_to)
                    )
    return lax.ppermute(shard, ("pipe", "ep"), pairs)


def picks(routes, expert, capacity):
    count = routes.shape[1]
    match = (routes == expert).astype(jnp.float32)
    upto = (
        lax.broadcasted_iota(jnp.int32, (count, count), 0)
        <= lax.broadcasted_iota(jnp.int32, (count, count), 1)
    ).astype(jnp.float32)
    rank = jnp.dot(match, upto, preferred_element_type=jnp.float32)
    slots = lax.broadcasted_iota(jnp.int32, (capacity, count), 0).astype(jnp.float32) + 1.0
    return jnp.where((rank == slots) & (match > 0.0), 1.0, 0.0)


def slices_kernel(x_ref, down, *refs):
    outs, sems = refs[:-1], refs[-1]
    columns = outs[0].shape[1]
    copies = []
    for at, (offset, out) in enumerate(zip(OFFSETS, outs)):
        start = pl.multiple_of(lax.rem(x_ref[0] - offset + RING, RING) * columns, 128)
        copies.append(
            pltpu.make_async_copy(down.at[:, pl.ds(start, columns)], out, sems.at[at])
        )
    for copy in copies:
        copy.start()
    for copy in copies:
        copy.wait()


def slices(x, down):
    depth, width = down.shape
    return pl.pallas_call(
        slices_kernel,
        in_specs=[
            pl.BlockSpec(memory_space=pltpu.SMEM),
            pl.BlockSpec(memory_space=pltpu.HBM),
        ],
        out_specs=[pl.BlockSpec(memory_space=pltpu.VMEM)] * RING,
        out_shape=[jax.ShapeDtypeStruct((depth, width // RING), down.dtype)] * RING,
        scratch_shapes=[pltpu.SemaphoreType.DMA((RING,))],
        compiler_params=pltpu.CompilerParams(vmem_limit_bytes=VMEM_LIMIT),
        name="slices",
    )(x, pltpu.with_memory_space_constraint(down, pltpu.HBM))


def pack_kernel(place, fr, rr, fs, rs, fx, rx, *refs):
    (own_f, own_r, oth, fr_v, rr_v, fs_v, rs_v, fx_v, rx_v, sems) = refs
    count, width = fx.shape
    capacity = count // EXPERTS
    copies = [
        pltpu.make_async_copy(source, target, sems.at[at])
        for at, (source, target) in enumerate(
            ((fr, fr_v), (rr, rr_v), (fs, fs_v), (rs, rs_v), (fx, fx_v), (rx, rx_v))
        )
    ]
    for copy in copies:
        copy.start()
    mine, z = place[0], place[1]
    every = fr.shape[1]
    lane = lax.broadcasted_iota(jnp.int32, (capacity, 128), 1)
    token = lax.broadcasted_iota(jnp.int32, (capacity, count), 1).astype(jnp.float32)
    local = (
        lax.broadcasted_iota(jnp.int32, (every, count), 0)
        == lax.broadcasted_iota(jnp.int32, (every, count), 1) + mine * count
    ).astype(jnp.bfloat16)
    for copy in copies[:4]:
        copy.wait()
    found = []
    for routes, share in ((fr_v, fs_v), (rr_v, rs_v)):
        routes = jnp.dot(
            routes[...].astype(jnp.bfloat16), local, preferred_element_type=jnp.float32
        )
        routes = (routes > 0.5).astype(jnp.int32)
        for expert in (z, 1 - z):
            pick = picks(routes, expert, capacity)
            rest = jnp.sum(pick * share[...], axis=1, keepdims=True)
            tail = jnp.where(lane == 3, jnp.sum(pick * token, axis=1, keepdims=True), 0.0)
            for at_term in range(3):
                term = rest.astype(jnp.bfloat16).astype(jnp.float32)
                tail = jnp.where(lane == at_term, term, tail)
                rest = rest - term
            found.append((pick.astype(jnp.bfloat16), tail.astype(jnp.bfloat16)))
    for at, rows in enumerate((fx_v, rx_v)):
        copies[4 + at].wait()
        for side in range(2):
            pick, tail = found[2 * at + side]
            out = oth if side else (own_f, own_r)[at]
            part = slice(at * capacity, (at + 1) * capacity) if side else slice(None)
            out[part, :width] = jnp.dot(
                pick, rows[...], preferred_element_type=jnp.float32
            ).astype(jnp.bfloat16)
            out[part, width:] = tail


def pack(place, *arrays):
    count, width = arrays[4].shape
    every = arrays[0].shape[1]
    return pl.pallas_call(
        pack_kernel,
        in_specs=[pl.BlockSpec(memory_space=pltpu.SMEM)]
        + [pl.BlockSpec(memory_space=pltpu.HBM)] * 6,
        out_specs=[pl.BlockSpec(memory_space=pltpu.VMEM)] * 3,
        out_shape=[
            jax.ShapeDtypeStruct((rows, width + 128), jnp.bfloat16)
            for rows in (count // 2, count // 2, count)
        ],
        scratch_shapes=[pltpu.VMEM((1, every), jnp.int32)] * 2
        + [pltpu.VMEM((1, count), jnp.float32)] * 2
        + [pltpu.VMEM((count, width), jnp.bfloat16)] * 2
        + [pltpu.SemaphoreType.DMA((6,))],
        compiler_params=pltpu.CompilerParams(vmem_limit_bytes=VMEM_LIMIT),
        name="pack",
    )(place, *[pltpu.with_memory_space_constraint(a, pltpu.HBM) for a in arrays])


def planned(refs, plan, lanes):
    return jnp.concatenate([refs[a][start : start + n, lanes] for a, start, n in plan], axis=0)


def hidden_kernel(steps, plan, *refs):
    rows, (go, gt, uo, ut), (out, gated, upward) = refs[:-7], refs[-7:-3], refs[-3:]
    block = go.shape[0] // steps

    def step(at, _):
        part = pl.ds(pl.multiple_of(at * block, 128), block)
        x = planned(rows, plan, part)
        g = jnp.concatenate([go[part, :], gt[part, :]], axis=1)
        u = jnp.concatenate([uo[part, :], ut[part, :]], axis=1)
        gated[...] += jnp.dot(x, g, preferred_element_type=jnp.float32)
        upward[...] += jnp.dot(x, u, preferred_element_type=jnp.float32)
        return 0

    gated[...] = jnp.zeros_like(gated)
    upward[...] = jnp.zeros_like(upward)
    lax.fori_loop(0, steps, step, 0, unroll=True)
    out[...] = (jax.nn.silu(gated[...]) * upward[...]).astype(jnp.bfloat16)


def hidden_rows(rows, plan, weights):
    width, lanes = weights[0].shape
    count = sum(n for _, _, n in plan)
    whole = pl.BlockSpec(memory_space=pltpu.VMEM)
    return pl.pallas_call(
        functools.partial(hidden_kernel, 7, plan),
        in_specs=[whole] * (len(rows) + 4),
        out_specs=whole,
        out_shape=jax.ShapeDtypeStruct((count, 2 * lanes), jnp.bfloat16),
        scratch_shapes=[pltpu.VMEM((count, 2 * lanes), jnp.float32)] * 2,
        compiler_params=pltpu.CompilerParams(vmem_limit_bytes=VMEM_LIMIT),
        cost_estimate=pl.CostEstimate(
            flops=8 * count * width * lanes,
            bytes_accessed=2 * width * (count + 4 * lanes),
            transcendentals=count * 2 * lanes,
        ),
        name="hidden",
    )(*rows, *weights)


def out_kernel(steps, plan, x_ref, *refs):
    rows, hidden, down, outs, h = refs[:-11], refs[-11:-7], refs[-7:-5], refs[-5:-1], refs[-1]
    pair = outs[0].shape[0]
    lanes = hidden[0].shape[1] // 2
    columns = down[0].shape[1]
    width = RING * columns
    block = columns // steps
    for at, o in enumerate(OFFSETS):
        for core in range(CORES):
            for index, (s, source) in enumerate(zip(OFFSETS, hidden)):
                place = PLACE[(o - s) % RING]
                h[
                    at * pair : (at + 1) * pair,
                    (core * RING + index) * lanes : (core * RING + index + 1) * lanes,
                ] = source[place * pair : (place + 1) * pair, core * lanes : (core + 1) * lanes]
    terms = planned(rows, plan, slice(width, None)).astype(jnp.float32)
    share = terms[:, 0:1] + terms[:, 1:2] + terms[:, 2:3]

    def step(j, _):
        part = pl.ds(pl.multiple_of(j * block, 128), block)
        there = pl.ds(pl.multiple_of(x_ref[0] * columns + j * block, 128), block)
        d = jnp.concatenate([r[:, part] for r in down], axis=0)
        branch = jnp.dot(h[...], d, preferred_element_type=jnp.float32)
        states = planned(rows, plan, there).astype(jnp.float32)
        result = (states + share * branch).astype(jnp.bfloat16)
        for at, out in enumerate(outs):
            out[:, part] = result[at * pair : (at + 1) * pair]
        return 0

    lax.fori_loop(0, steps, step, 0, unroll=True)


def out_rows(x, rows, plan, hidden, down):
    wide = rows[0].shape[1]
    count = sum(n for _, _, n in plan)
    pair = count // RING
    columns = (wide - 128) // RING
    lanes = hidden[0].shape[1]
    whole = pl.BlockSpec(memory_space=pltpu.VMEM)
    return pl.pallas_call(
        functools.partial(out_kernel, 7, plan),
        in_specs=[pl.BlockSpec(memory_space=pltpu.SMEM)] + [whole] * (len(rows) + 6),
        out_specs=[whole] * 4,
        out_shape=[jax.ShapeDtypeStruct((pair, columns), jnp.bfloat16)] * 4,
        scratch_shapes=[pltpu.VMEM((count, RING * lanes), jnp.bfloat16)],
        compiler_params=pltpu.CompilerParams(vmem_limit_bytes=VMEM_LIMIT),
        cost_estimate=pl.CostEstimate(
            flops=2 * count * columns * 4 * lanes,
            bytes_accessed=2 * columns * (2 * count + 4 * lanes),
            transcendentals=0,
        ),
        name="out",
    )(x, *rows, *hidden, *down)


def stack_kernel(*refs):
    depth = refs[0].shape[0]
    for at, piece in enumerate(refs[:-1]):
        refs[-1][at * depth : (at + 1) * depth, :] = piece[...]


def stack(pieces):
    depth, columns = pieces[0].shape
    block = columns // 2
    return pl.pallas_call(
        stack_kernel,
        grid=(2,),
        in_specs=[pl.BlockSpec((depth, block), lambda j: (0, j))] * 4,
        out_specs=pl.BlockSpec((4 * depth, block), lambda j: (0, j)),
        out_shape=jax.ShapeDtypeStruct((4 * depth, columns), jnp.bfloat16),
        compiler_params=pltpu.CompilerParams(vmem_limit_bytes=VMEM_LIMIT),
        name="stack",
    )(*pieces)


def pairs_kernel(a, b, c, d, ab, cd):
    half = a.shape[0]
    ab[:half], ab[half:] = a[...], b[...]
    cd[:half], cd[half:] = c[...], d[...]


def pairs(*arrays):
    half, wide = arrays[0].shape
    whole = pl.BlockSpec(memory_space=pltpu.VMEM)
    return pl.pallas_call(
        pairs_kernel,
        in_specs=[whole] * 4,
        out_specs=[whole] * 2,
        out_shape=[jax.ShapeDtypeStruct((2 * half, wide), arrays[0].dtype)] * 2,
        compiler_params=pltpu.CompilerParams(vmem_limit_bytes=VMEM_LIMIT),
        name="pairs",
    )(*arrays)


def regroup_kernel(x_ref, *refs):
    tails, pieces, outs = refs[:-6], refs[-6:-2], refs[-2:]
    tails = jnp.concatenate([tail[...] for tail in tails], axis=0)
    pair, columns = pieces[0].shape
    capacity = pair // 2
    for direction, out in enumerate(outs):
        part = slice(direction * capacity, (direction + 1) * capacity)
        for offset, piece in zip(OFFSETS, pieces):
            start = pl.multiple_of(lax.rem(x_ref[0] - offset + RING, RING) * columns, 128)
            out[:, pl.ds(start, columns)] = piece[part, :]
        out[:, RING * columns :] = tails[part]


def regroup(x, rows, pieces):
    pair, columns = pieces[0].shape
    wide = RING * columns + 128
    whole = pl.BlockSpec((pair, columns), lambda j, x: (0, 0))
    return pl.pallas_call(
        regroup_kernel,
        grid_spec=pltpu.PrefetchScalarGridSpec(
            num_scalar_prefetch=1,
            grid=(1,),
            in_specs=[
                pl.BlockSpec((r.shape[0], 128), lambda j, x: (0, RING * columns // 128))
                for r in rows
            ]
            + [whole] * 4,
            out_specs=[pl.BlockSpec((pair // 2, wide), lambda j, x: (0, 0))] * 2,
        ),
        out_shape=[jax.ShapeDtypeStruct((pair // 2, wide), jnp.bfloat16)] * 2,
        compiler_params=pltpu.CompilerParams(vmem_limit_bytes=VMEM_LIMIT),
        name="regroup",
    )(x, *rows, *pieces)


def merge_kernel(*refs):
    pieces, outs = refs[:-2], refs[-2:]
    count, width = outs[0].shape
    token = lax.broadcasted_iota(jnp.int32, (count, count), 1).astype(jnp.float32)
    for direction, out in enumerate(outs):
        mine = pieces[direction::2]
        rows = jnp.concatenate([piece[:, :width] for piece in mine], axis=0)
        place = jnp.concatenate([piece[:, width:] for piece in mine], axis=0).astype(jnp.float32)
        pick = jnp.where(place[:, 3:4] == token, 1.0, 0.0).astype(jnp.bfloat16)
        out[...] = lax.dot_general(
            pick, rows, (((0,), (0,)), ((), ())), preferred_element_type=jnp.float32
        ).astype(jnp.bfloat16)


def merge(pieces):
    count = sum(piece.shape[0] for piece in pieces) // 2
    whole = pl.BlockSpec(memory_space=pltpu.VMEM)
    shape = jax.ShapeDtypeStruct((count, pieces[0].shape[1] - 128), jnp.bfloat16)
    return pl.pallas_call(
        merge_kernel,
        in_specs=[whole] * len(pieces),
        out_specs=[whole] * 2,
        out_shape=[shape] * 2,
        compiler_params=pltpu.CompilerParams(vmem_limit_bytes=VMEM_LIMIT),
        name="merge",
    )(*pieces)


def after(values, deps):
    return lax.optimization_barrier((tuple(values), tuple(deps)))[0]


def per_device(
    forward_states,
    reverse_states,
    forward_routes,
    reverse_routes,
    forward_share,
    reverse_share,
    layer_gate,
    layer_up,
    layer_down,
):
    pipes = lax.axis_size("pipe")
    send = functools.partial(move, pipes=pipes)
    mine = lax.axis_index("ep").astype(jnp.int32)
    z = mine // (RING * CORES)
    x = (mine // CORES) % RING
    count, width = forward_states.shape[1:]
    columns = width // RING
    gate, up, down = layer_gate[0], layer_up[0], layer_down[0]

    at_x = x[None]

    def spread(h):
        return [h] + [send(h, steps=-o) for o in OFFSETS[1:]]

    def back(outs):
        return [outs[0]] + [send(out, steps=o) for out, o in zip(outs[1:], OFFSETS[1:])]

    def first(f, r):
        return send(f, steps=1), send(r, steps=-1)

    with jax.named_scope("weights"):
        weights = [gate, send(gate, core=True), up, send(up, core=True)]

    with jax.named_scope("pack"):
        own_f, own_r, oth = pack(
            jnp.stack([mine, z]),
            forward_routes.reshape(1, -1),
            reverse_routes.reshape(1, -1),
            forward_share.reshape(1, count),
            reverse_share.reshape(1, count),
            forward_states[0],
            reverse_states[0],
        )
    half = count // 2
    with jax.named_scope("swap"):
        swapped = send(oth, flip=True)
    with jax.named_scope("first1"):
        own_left_f, own_right_r = first(own_f, own_r)

    with jax.named_scope("down"):
        parts = list(slices(after((at_x,), (own_f,))[0], down))
        parts[1:3] = after(parts[1:3], (weights[1], weights[3]))
        parts[1:3] = [send(part, steps=-o) for part, o in zip(parts[1:3], OFFSETS[1:3])]

        parts[3:] = after(parts[3:], (own_left_f, own_right_r))
        parts[3] = send(parts[3], steps=-OFFSETS[3])
    plan = (
        *((0, 0, half), (1, 0, half)),
        *((2, 0, half), (4, half, half)),
        *((5, half, half), (3, 0, half)),
        *((4, 0, half), (5, 0, half)),
    )

    def gather(f, r, left_f, right_r, dep):
        left_f, right_r = after((left_f, right_r), dep)
        onward, backward = pairs(left_f, r, right_r, f)
        onward, backward = send(onward, steps=1), send(backward, steps=-1)
        return [f, r, left_f, right_r, onward, backward]

    with jax.named_scope("second1"):
        rows1 = gather(own_f, own_r, own_left_f, own_right_r, [swapped] + parts[1:3])
    with jax.named_scope("down"):
        half_down = stack(parts)
        down = [half_down, send(half_down, core=True)]
    with jax.named_scope("first0"):
        (swapped,) = after((swapped,), parts[1:])
        f, r = swapped[:half], swapped[half:]
        left_f, right_r = first(f, r)
    with jax.named_scope("hidden1"):
        hidden1 = spread(hidden_rows(after(rows1, down[1:]), plan, weights))
    with jax.named_scope("second0"):
        rows0 = gather(f, r, left_f, right_r, hidden1[1:])
    with jax.named_scope("out1"):
        outs1 = out_rows(at_x, rows1, plan, hidden1, down)
    with jax.named_scope("back1"):
        back1 = back(outs1)
    with jax.named_scope("hidden0"):
        hidden0 = spread(hidden_rows(rows0, plan, weights))
    with jax.named_scope("relay1"):
        whole_f, whole_r = regroup(at_x, [own_f, own_r], after(back1, hidden0[:1]))
        sent1 = [send(whole_f, by=1), send(whole_r, by=-1)]
    with jax.named_scope("out0"):
        outs0 = out_rows(at_x, rows0, plan, hidden0, down)
    with jax.named_scope("back0"):
        back0 = back(outs0)
    with jax.named_scope("relay0"):
        whole_f, whole_r = regroup(at_x, [swapped], back0)
        sent0 = [send(whole_f, by=1, flip=True), send(whole_r, by=-1, flip=True)]
    with jax.named_scope("merge"):
        ahead, behind = merge(sent1 + sent0)
    return (ahead[None], behind[None])


def solution(mesh):
    in_specs = (
        P("pipe", "ep", None),
        P("pipe", "ep", None),
        P(None, "pipe", None, None),
        P(None, "pipe", None, None),
        P(None, "pipe", "ep"),
        P(None, "pipe", "ep"),
        P("pipe", None, "ep"),
        P("pipe", None, "ep"),
        P("pipe", "ep", None),
    )
    out_specs = (P("pipe", "ep", None), P("pipe", "ep", None))
    return jax.shard_map(
        per_device, mesh=mesh, in_specs=in_specs, out_specs=out_specs, check_vma=False
    )
```

```python
import functools

import jax
import jax.numpy as jnp
from jax import lax
from jax.experimental import pallas as pl
from jax.experimental.pallas import tpu as pltpu
from jax.sharding import PartitionSpec as P

EXPERTS = 2
RING = 4
CORES = 2
OFFSETS = (0, -1, 1, 2)
PLACE = {offset % RING: at for at, offset in enumerate(OFFSETS)}
VMEM_LIMIT = 16 * 1024 * 1024


def move(shard, pipes, by=0, flip=False, steps=0, core=False):
    pairs = []
    for pipe in range(pipes):
        if not 0 <= pipe + by < pipes:
            continue
        for z in range(EXPERTS):
            for x in range(RING):
                for c in range(CORES):
                    source = ((pipe * EXPERTS + z) * RING + x) * CORES + c
                    z_to = 1 - z if flip else z
                    x_to = (x + steps) % RING
                    c_to = 1 - c if core else c
                    pairs.append(
                        (source, (((pipe + by) * EXPERTS + z_to) * RING + x_to) * CORES + c_to)
                    )
    return lax.ppermute(shard, ("pipe", "ep"), pairs)


def slices_kernel(x_ref, down, *refs):
    outs, sems = refs[:-1], refs[-1]
    columns = outs[0].shape[1]
    copies = []
    for at, (offset, out) in enumerate(zip(OFFSETS, outs)):
        start = pl.multiple_of(lax.rem(x_ref[0] - offset + RING, RING) * columns, 128)
        copies.append(
            pltpu.make_async_copy(down.at[:, pl.ds(start, columns)], out, sems.at[at])
        )
    for copy in copies:
        copy.start()
    for copy in copies:
        copy.wait()


def slices(x, down):
    depth, width = down.shape
    return pl.pallas_call(
        slices_kernel,
        in_specs=[
            pl.BlockSpec(memory_space=pltpu.SMEM),
            pl.BlockSpec(memory_space=pltpu.HBM),
        ],
        out_specs=[pl.BlockSpec(memory_space=pltpu.VMEM)] * RING,
        out_shape=[jax.ShapeDtypeStruct((depth, width // RING), down.dtype)] * RING,
        scratch_shapes=[pltpu.SemaphoreType.DMA((RING,))],
        compiler_params=pltpu.CompilerParams(vmem_limit_bytes=VMEM_LIMIT),
        name="slices",
    )(x, pltpu.with_memory_space_constraint(down, pltpu.HBM))


def pack_kernel(place, fr, rr, fs, rs, fx, rx, *refs):
    (own_f, own_r, oth, fr_v, rr_v, fs_v, rs_v, fx_v, rx_v, sems) = refs
    count, width = fx.shape
    capacity = count // EXPERTS
    copies = [
        pltpu.make_async_copy(source, target, sems.at[at])
        for at, (source, target) in enumerate(
            ((fr, fr_v), (rr, rr_v), (fs, fs_v), (rs, rs_v), (fx, fx_v), (rx, rx_v))
        )
    ]
    for copy in copies:
        copy.start()
    mine, z = place[0], place[1]
    every = fr.shape[1]
    lane = lax.broadcasted_iota(jnp.int32, (count, 128), 1)
    token = lax.broadcasted_iota(jnp.int32, (count, count), 1).astype(jnp.float32)
    local = (
        lax.broadcasted_iota(jnp.int32, (every, count), 0)
        == lax.broadcasted_iota(jnp.int32, (every, count), 1) + mine * count
    ).astype(jnp.bfloat16)
    for copy in copies[:4]:
        copy.wait()
    upto = (
        lax.broadcasted_iota(jnp.int32, (count, count), 0)
        <= lax.broadcasted_iota(jnp.int32, (count, count), 1)
    ).astype(jnp.bfloat16)
    row = lax.broadcasted_iota(jnp.int32, (count, count), 0)
    wanted = jnp.where(row < capacity, z, 1 - z).astype(jnp.float32)
    slot = (jnp.where(row < capacity, row, row - capacity) + 1).astype(jnp.float32)
    found = []
    for routes, share in ((fr_v, fs_v), (rr_v, rs_v)):
        routes = jnp.dot(
            routes[...].astype(jnp.bfloat16), local, preferred_element_type=jnp.float32
        )
        match = jnp.broadcast_to(routes, (count, count)) == wanted
        rank = jnp.dot(
            jnp.where(match, 1.0, 0.0).astype(jnp.bfloat16),
            upto,
            preferred_element_type=jnp.float32,
        )
        pick = jnp.where(match & (rank == slot), 1.0, 0.0)
        rest = jnp.sum(pick * share[...], axis=1, keepdims=True)
        tail = jnp.where(lane == 3, jnp.sum(pick * token, axis=1, keepdims=True), 0.0)
        for at_term in range(3):
            term = rest.astype(jnp.bfloat16).astype(jnp.float32)
            tail = jnp.where(lane == at_term, term, tail)
            rest = rest - term
        found.append((pick.astype(jnp.bfloat16), tail.astype(jnp.bfloat16)))
    for at, rows in enumerate((fx_v, rx_v)):
        copies[4 + at].wait()
        pick, tail = found[at]
        own = (own_f, own_r)[at]
        part = slice(at * capacity, (at + 1) * capacity)
        both = jnp.dot(pick, rows[...], preferred_element_type=jnp.float32).astype(jnp.bfloat16)
        own[:, :width], oth[part, :width] = both[:capacity], both[capacity:]
        own[:, width:], oth[part, width:] = tail[:capacity], tail[capacity:]


def pack(place, *arrays):
    count, width = arrays[4].shape
    every = arrays[0].shape[1]
    return pl.pallas_call(
        pack_kernel,
        in_specs=[pl.BlockSpec(memory_space=pltpu.SMEM)]
        + [pl.BlockSpec(memory_space=pltpu.HBM)] * 6,
        out_specs=[pl.BlockSpec(memory_space=pltpu.VMEM)] * 3,
        out_shape=[
            jax.ShapeDtypeStruct((rows, width + 128), jnp.bfloat16)
            for rows in (count // 2, count // 2, count)
        ],
        scratch_shapes=[pltpu.VMEM((1, every), jnp.int32)] * 2
        + [pltpu.VMEM((1, count), jnp.float32)] * 2
        + [pltpu.VMEM((count, width), jnp.bfloat16)] * 2
        + [pltpu.SemaphoreType.DMA((6,))],
        compiler_params=pltpu.CompilerParams(vmem_limit_bytes=VMEM_LIMIT),
        name="pack",
    )(place, *[pltpu.with_memory_space_constraint(a, pltpu.HBM) for a in arrays])


def planned(refs, plan, lanes):
    return jnp.concatenate([refs[a][start : start + n, lanes] for a, start, n in plan], axis=0)


def hidden_kernel(steps, plan, *refs):
    rows, (go, gt, uo, ut), (out, gated, upward) = refs[:-7], refs[-7:-3], refs[-3:]
    block = go.shape[0] // steps

    def step(at, _):
        part = pl.ds(pl.multiple_of(at * block, 128), block)
        x = planned(rows, plan, part)
        g = jnp.concatenate([go[part, :], gt[part, :]], axis=1)
        u = jnp.concatenate([uo[part, :], ut[part, :]], axis=1)
        gated[...] += jnp.dot(x, g, preferred_element_type=jnp.float32)
        upward[...] += jnp.dot(x, u, preferred_element_type=jnp.float32)
        return 0

    gated[...] = jnp.zeros_like(gated)
    upward[...] = jnp.zeros_like(upward)
    lax.fori_loop(0, steps, step, 0, unroll=True)
    out[...] = (jax.nn.silu(gated[...]) * upward[...]).astype(jnp.bfloat16)


def hidden_rows(rows, plan, weights):
    width, lanes = weights[0].shape
    count = sum(n for _, _, n in plan)
    whole = pl.BlockSpec(memory_space=pltpu.VMEM)
    return pl.pallas_call(
        functools.partial(hidden_kernel, 7, plan),
        in_specs=[whole] * (len(rows) + 4),
        out_specs=whole,
        out_shape=jax.ShapeDtypeStruct((count, 2 * lanes), jnp.bfloat16),
        scratch_shapes=[pltpu.VMEM((count, 2 * lanes), jnp.float32)] * 2,
        compiler_params=pltpu.CompilerParams(vmem_limit_bytes=VMEM_LIMIT),
        cost_estimate=pl.CostEstimate(
            flops=8 * count * width * lanes,
            bytes_accessed=2 * width * (count + 4 * lanes),
            transcendentals=count * 2 * lanes,
        ),
        name="hidden",
    )(*rows, *weights)


def out_kernel(steps, plan, x_ref, *refs):
    rows, hidden, down, outs, h = refs[:-11], refs[-11:-7], refs[-7:-5], refs[-5:-1], refs[-1]
    pair = outs[0].shape[0]
    lanes = hidden[0].shape[1] // 2
    columns = down[0].shape[1]
    width = RING * columns
    block = columns // steps
    for at, o in enumerate(OFFSETS):
        for core in range(CORES):
            for index, (s, source) in enumerate(zip(OFFSETS, hidden)):
                place = PLACE[(o - s) % RING]
                h[
                    at * pair : (at + 1) * pair,
                    (core * RING + index) * lanes : (core * RING + index + 1) * lanes,
                ] = source[place * pair : (place + 1) * pair, core * lanes : (core + 1) * lanes]
    terms = planned(rows, plan, slice(width, None)).astype(jnp.float32)
    share = terms[:, 0:1] + terms[:, 1:2] + terms[:, 2:3]

    def step(j, _):
        part = pl.ds(pl.multiple_of(j * block, 128), block)
        there = pl.ds(pl.multiple_of(x_ref[0] * columns + j * block, 128), block)
        d = jnp.concatenate([r[:, part] for r in down], axis=0)
        branch = jnp.dot(h[...], d, preferred_element_type=jnp.float32)
        states = planned(rows, plan, there).astype(jnp.float32)
        result = (states + share * branch).astype(jnp.bfloat16)
        for at, out in enumerate(outs):
            out[:, part] = result[at * pair : (at + 1) * pair]
        return 0

    lax.fori_loop(0, steps, step, 0, unroll=True)


def out_rows(x, rows, plan, hidden, down):
    wide = rows[0].shape[1]
    count = sum(n for _, _, n in plan)
    pair = count // RING
    columns = (wide - 128) // RING
    lanes = hidden[0].shape[1]
    whole = pl.BlockSpec(memory_space=pltpu.VMEM)
    return pl.pallas_call(
        functools.partial(out_kernel, 7, plan),
        in_specs=[pl.BlockSpec(memory_space=pltpu.SMEM)] + [whole] * (len(rows) + 6),
        out_specs=[whole] * 4,
        out_shape=[jax.ShapeDtypeStruct((pair, columns), jnp.bfloat16)] * 4,
        scratch_shapes=[pltpu.VMEM((count, RING * lanes), jnp.bfloat16)],
        compiler_params=pltpu.CompilerParams(vmem_limit_bytes=VMEM_LIMIT),
        cost_estimate=pl.CostEstimate(
            flops=2 * count * columns * 4 * lanes,
            bytes_accessed=2 * columns * (2 * count + 4 * lanes),
            transcendentals=0,
        ),
        name="out",
    )(x, *rows, *hidden, *down)


def stack_kernel(*refs):
    depth = refs[0].shape[0]
    for at, piece in enumerate(refs[:-1]):
        refs[-1][at * depth : (at + 1) * depth, :] = piece[...]


def stack(pieces):
    depth, columns = pieces[0].shape
    block = columns // 2
    return pl.pallas_call(
        stack_kernel,
        grid=(2,),
        in_specs=[pl.BlockSpec((depth, block), lambda j: (0, j))] * 4,
        out_specs=pl.BlockSpec((4 * depth, block), lambda j: (0, j)),
        out_shape=jax.ShapeDtypeStruct((4 * depth, columns), jnp.bfloat16),
        compiler_params=pltpu.CompilerParams(vmem_limit_bytes=VMEM_LIMIT),
        name="stack",
    )(*pieces)


def pairs_kernel(a, b, c, d, ab, cd):
    half = a.shape[0]
    ab[:half], ab[half:] = a[...], b[...]
    cd[:half], cd[half:] = c[...], d[...]


def pairs(*arrays):
    half, wide = arrays[0].shape
    whole = pl.BlockSpec(memory_space=pltpu.VMEM)
    return pl.pallas_call(
        pairs_kernel,
        in_specs=[whole] * 4,
        out_specs=[whole] * 2,
        out_shape=[jax.ShapeDtypeStruct((2 * half, wide), arrays[0].dtype)] * 2,
        compiler_params=pltpu.CompilerParams(vmem_limit_bytes=VMEM_LIMIT),
        name="pairs",
    )(*arrays)


def regroup_kernel(x_ref, *refs):
    tails, pieces, outs = refs[:-6], refs[-6:-2], refs[-2:]
    tails = jnp.concatenate([tail[...] for tail in tails], axis=0)
    pair, columns = pieces[0].shape
    capacity = pair // 2
    for direction, out in enumerate(outs):
        part = slice(direction * capacity, (direction + 1) * capacity)
        for offset, piece in zip(OFFSETS, pieces):
            start = pl.multiple_of(lax.rem(x_ref[0] - offset + RING, RING) * columns, 128)
            out[:, pl.ds(start, columns)] = piece[part, :]
        out[:, RING * columns :] = tails[part]


def regroup(x, rows, pieces):
    pair, columns = pieces[0].shape
    wide = RING * columns + 128
    whole = pl.BlockSpec((pair, columns), lambda j, x: (0, 0))
    return pl.pallas_call(
        regroup_kernel,
        grid_spec=pltpu.PrefetchScalarGridSpec(
            num_scalar_prefetch=1,
            grid=(1,),
            in_specs=[
                pl.BlockSpec((r.shape[0], 128), lambda j, x: (0, RING * columns // 128))
                for r in rows
            ]
            + [whole] * 4,
            out_specs=[pl.BlockSpec((pair // 2, wide), lambda j, x: (0, 0))] * 2,
        ),
        out_shape=[jax.ShapeDtypeStruct((pair // 2, wide), jnp.bfloat16)] * 2,
        compiler_params=pltpu.CompilerParams(vmem_limit_bytes=VMEM_LIMIT),
        name="regroup",
    )(x, *rows, *pieces)


def merge_kernel(*refs):
    pieces, outs = refs[:-2], refs[-2:]
    count, width = outs[0].shape
    token = lax.broadcasted_iota(jnp.int32, (count, count), 1).astype(jnp.float32)
    for direction, out in enumerate(outs):
        mine = pieces[direction::2]
        rows = jnp.concatenate([piece[:, :width] for piece in mine], axis=0)
        place = jnp.concatenate([piece[:, width:] for piece in mine], axis=0).astype(jnp.float32)
        pick = jnp.where(place[:, 3:4] == token, 1.0, 0.0).astype(jnp.bfloat16)
        out[...] = lax.dot_general(
            pick, rows, (((0,), (0,)), ((), ())), preferred_element_type=jnp.float32
        ).astype(jnp.bfloat16)


def merge(pieces):
    count = sum(piece.shape[0] for piece in pieces) // 2
    whole = pl.BlockSpec(memory_space=pltpu.VMEM)
    shape = jax.ShapeDtypeStruct((count, pieces[0].shape[1] - 128), jnp.bfloat16)
    return pl.pallas_call(
        merge_kernel,
        in_specs=[whole] * len(pieces),
        out_specs=[whole] * 2,
        out_shape=[shape] * 2,
        compiler_params=pltpu.CompilerParams(vmem_limit_bytes=VMEM_LIMIT),
        name="merge",
    )(*pieces)


def after(values, deps):
    return lax.optimization_barrier((tuple(values), tuple(deps)))[0]


def per_device(
    forward_states,
    reverse_states,
    forward_routes,
    reverse_routes,
    forward_share,
    reverse_share,
    layer_gate,
    layer_up,
    layer_down,
):
    pipes = lax.axis_size("pipe")
    send = functools.partial(move, pipes=pipes)
    mine = lax.axis_index("ep").astype(jnp.int32)
    z = mine // (RING * CORES)
    x = (mine // CORES) % RING
    count, width = forward_states.shape[1:]
    columns = width // RING
    gate, up, down = layer_gate[0], layer_up[0], layer_down[0]

    at_x = x[None]

    def spread(h):
        return [h] + [send(h, steps=-o) for o in OFFSETS[1:]]

    def back(outs):
        return [outs[0]] + [send(out, steps=o) for out, o in zip(outs[1:], OFFSETS[1:])]

    def first(f, r):
        return send(f, steps=1), send(r, steps=-1)

    with jax.named_scope("weights"):
        weights = [gate, send(gate, core=True), up, send(up, core=True)]

    with jax.named_scope("pack"):
        own_f, own_r, oth = pack(
            jnp.stack([mine, z]),
            forward_routes.reshape(1, -1),
            reverse_routes.reshape(1, -1),
            forward_share.reshape(1, count),
            reverse_share.reshape(1, count),
            forward_states[0],
            reverse_states[0],
        )
    half = count // 2
    with jax.named_scope("swap"):
        swapped = send(oth, flip=True)
    with jax.named_scope("first1"):
        own_left_f, own_right_r = first(own_f, own_r)

    with jax.named_scope("down"):
        parts = list(slices(after((at_x,), (own_f,))[0], down))
        parts[1:3] = after(parts[1:3], (weights[1], weights[3]))
        parts[1:3] = [send(part, steps=-o) for part, o in zip(parts[1:3], OFFSETS[1:3])]

        parts[3:] = after(parts[3:], (own_left_f, own_right_r))
        parts[3] = send(parts[3], steps=-OFFSETS[3])
    plan = (
        *((0, 0, half), (1, 0, half)),
        *((2, 0, half), (4, half, half)),
        *((5, half, half), (3, 0, half)),
        *((4, 0, half), (5, 0, half)),
    )

    def gather(f, r, left_f, right_r, dep):
        left_f, right_r = after((left_f, right_r), dep)
        onward, backward = pairs(left_f, r, right_r, f)
        onward, backward = send(onward, steps=1), send(backward, steps=-1)
        return [f, r, left_f, right_r, onward, backward]

    with jax.named_scope("second1"):
        rows1 = gather(own_f, own_r, own_left_f, own_right_r, parts[1:3])
    with jax.named_scope("down"):
        half_down = stack(parts)
        down = [half_down, send(half_down, core=True)]
    with jax.named_scope("first0"):
        (swapped,) = after((swapped,), parts[1:])
        f, r = swapped[:half], swapped[half:]
        left_f, right_r = first(f, r)
    with jax.named_scope("hidden1"):
        hidden1 = spread(hidden_rows(after(rows1, down[1:]), plan, weights))
    with jax.named_scope("second0"):
        rows0 = gather(f, r, left_f, right_r, hidden1[1:])
    with jax.named_scope("out1"):
        outs1 = out_rows(at_x, rows1, plan, hidden1, down)
    with jax.named_scope("back1"):
        back1 = back(outs1)
    with jax.named_scope("hidden0"):
        hidden0 = spread(hidden_rows(rows0, plan, weights))
    with jax.named_scope("relay1"):
        whole_f, whole_r = regroup(at_x, [own_f, own_r], after(back1, hidden0[:1]))
        sent1 = [send(whole_f, by=1), send(whole_r, by=-1)]
    with jax.named_scope("out0"):
        outs0 = out_rows(at_x, rows0, plan, hidden0, down)
    with jax.named_scope("back0"):
        back0 = back(outs0)
    with jax.named_scope("relay0"):
        whole_f, whole_r = regroup(at_x, [swapped], back0)
        sent0 = [send(whole_f, by=1, flip=True), send(whole_r, by=-1, flip=True)]
    with jax.named_scope("merge"):
        ahead, behind = merge(sent1 + sent0)
    return (ahead[None], behind[None])


def solution(mesh):
    in_specs = (
        P("pipe", "ep", None),
        P("pipe", "ep", None),
        P(None, "pipe", None, None),
        P(None, "pipe", None, None),
        P(None, "pipe", "ep"),
        P(None, "pipe", "ep"),
        P("pipe", None, "ep"),
        P("pipe", None, "ep"),
        P("pipe", "ep", None),
    )
    out_specs = (P("pipe", "ep", None), P("pipe", "ep", None))
    return jax.shard_map(
        per_device, mesh=mesh, in_specs=in_specs, out_specs=out_specs, check_vma=False
    )
```

```python
import functools

import jax
import jax.numpy as jnp
from jax import lax
from jax.experimental import pallas as pl
from jax.experimental.pallas import tpu as pltpu
from jax.sharding import PartitionSpec as P

EXPERTS = 2
RING = 4
CORES = 2
OFFSETS = (0, -1, 1, 2)
PLACE = {offset % RING: at for at, offset in enumerate(OFFSETS)}
VMEM_LIMIT = 16 * 1024 * 1024


def move(shard, pipes, by=0, flip=False, steps=0, core=False):
    pairs = []
    for pipe in range(pipes):
        if not 0 <= pipe + by < pipes:
            continue
        for z in range(EXPERTS):
            for x in range(RING):
                for c in range(CORES):
                    source = ((pipe * EXPERTS + z) * RING + x) * CORES + c
                    z_to = 1 - z if flip else z
                    x_to = (x + steps) % RING
                    c_to = 1 - c if core else c
                    pairs.append(
                        (source, (((pipe + by) * EXPERTS + z_to) * RING + x_to) * CORES + c_to)
                    )
    return lax.ppermute(shard, ("pipe", "ep"), pairs)


def slices_kernel(x_ref, down, *refs):
    outs, sems = refs[:-1], refs[-1]
    columns = outs[0].shape[1]
    copies = []
    for at, (offset, out) in enumerate(zip(OFFSETS, outs)):
        start = pl.multiple_of(lax.rem(x_ref[0] - offset + RING, RING) * columns, 128)
        copies.append(
            pltpu.make_async_copy(down.at[:, pl.ds(start, columns)], out, sems.at[at])
        )
    for copy in copies:
        copy.start()
    for copy in copies:
        copy.wait()


def slices(x, down):
    depth, width = down.shape
    return pl.pallas_call(
        slices_kernel,
        in_specs=[
            pl.BlockSpec(memory_space=pltpu.SMEM),
            pl.BlockSpec(memory_space=pltpu.HBM),
        ],
        out_specs=[pl.BlockSpec(memory_space=pltpu.VMEM)] * RING,
        out_shape=[jax.ShapeDtypeStruct((depth, width // RING), down.dtype)] * RING,
        scratch_shapes=[pltpu.SemaphoreType.DMA((RING,))],
        compiler_params=pltpu.CompilerParams(vmem_limit_bytes=VMEM_LIMIT),
        name="slices",
    )(x, pltpu.with_memory_space_constraint(down, pltpu.HBM))


def pack_kernel(place, fr, rr, fs, rs, fx, rx, *refs):
    (own_f, own_r, oth, fr_v, rr_v, fs_v, rs_v, fx_v, rx_v, sems) = refs
    count, width = fx.shape
    capacity = count // EXPERTS
    copies = [
        pltpu.make_async_copy(source, target, sems.at[at])
        for at, (source, target) in enumerate(
            ((fr, fr_v), (rr, rr_v), (fs, fs_v), (rs, rs_v), (fx, fx_v), (rx, rx_v))
        )
    ]
    for copy in copies:
        copy.start()
    mine, z = place[0], place[1]
    every = fr.shape[1]
    lane = lax.broadcasted_iota(jnp.int32, (count, 128), 1)
    token = lax.broadcasted_iota(jnp.int32, (count, count), 1).astype(jnp.float32)
    local = (
        lax.broadcasted_iota(jnp.int32, (every, count), 0)
        == lax.broadcasted_iota(jnp.int32, (every, count), 1) + mine * count
    ).astype(jnp.bfloat16)
    for copy in copies[:4]:
        copy.wait()
    upto = (
        lax.broadcasted_iota(jnp.int32, (count, count), 0)
        <= lax.broadcasted_iota(jnp.int32, (count, count), 1)
    ).astype(jnp.bfloat16)
    row = lax.broadcasted_iota(jnp.int32, (count, count), 0)
    wanted = jnp.where(row < capacity, z, 1 - z).astype(jnp.float32)
    slot = (jnp.where(row < capacity, row, row - capacity) + 1).astype(jnp.float32)
    found = []
    for routes, share in ((fr_v, fs_v), (rr_v, rs_v)):
        routes = jnp.dot(
            routes[...].astype(jnp.bfloat16), local, preferred_element_type=jnp.float32
        )
        match = jnp.broadcast_to(routes, (count, count)) == wanted
        rank = jnp.dot(
            jnp.where(match, 1.0, 0.0).astype(jnp.bfloat16),
            upto,
            preferred_element_type=jnp.float32,
        )
        pick = jnp.where(match & (rank == slot), 1.0, 0.0)
        rest = jnp.sum(pick * share[...], axis=1, keepdims=True)
        tail = jnp.where(lane == 3, jnp.sum(pick * token, axis=1, keepdims=True), 0.0)
        for at_term in range(3):
            term = rest.astype(jnp.bfloat16).astype(jnp.float32)
            tail = jnp.where(lane == at_term, term, tail)
            rest = rest - term
        found.append((pick.astype(jnp.bfloat16), tail.astype(jnp.bfloat16)))
    for at, rows in enumerate((fx_v, rx_v)):
        copies[4 + at].wait()
        pick, tail = found[at]
        own = (own_f, own_r)[at]
        part = slice(at * capacity, (at + 1) * capacity)
        both = jnp.dot(pick, rows[...], preferred_element_type=jnp.float32).astype(jnp.bfloat16)
        own[:, :width], oth[part, :width] = both[:capacity], both[capacity:]
        own[:, width:], oth[part, width:] = tail[:capacity], tail[capacity:]


def pack(place, *arrays):
    count, width = arrays[4].shape
    every = arrays[0].shape[1]
    return pl.pallas_call(
        pack_kernel,
        in_specs=[pl.BlockSpec(memory_space=pltpu.SMEM)]
        + [pl.BlockSpec(memory_space=pltpu.HBM)] * 6,
        out_specs=[pl.BlockSpec(memory_space=pltpu.VMEM)] * 3,
        out_shape=[
            jax.ShapeDtypeStruct((rows, width + 128), jnp.bfloat16)
            for rows in (count // 2, count // 2, count)
        ],
        scratch_shapes=[pltpu.VMEM((1, every), jnp.int32)] * 2
        + [pltpu.VMEM((1, count), jnp.float32)] * 2
        + [pltpu.VMEM((count, width), jnp.bfloat16)] * 2
        + [pltpu.SemaphoreType.DMA((6,))],
        compiler_params=pltpu.CompilerParams(vmem_limit_bytes=VMEM_LIMIT),
        name="pack",
    )(place, *[pltpu.with_memory_space_constraint(a, pltpu.HBM) for a in arrays])


def planned(refs, plan, lanes):
    return jnp.concatenate([refs[a][start : start + n, lanes] for a, start, n in plan], axis=0)


def hidden_kernel(steps, plan, *refs):
    rows, (go, gt, uo, ut), (out, gated, upward) = refs[:-7], refs[-7:-3], refs[-3:]
    block = go.shape[0] // steps

    def step(at, _):
        part = pl.ds(pl.multiple_of(at * block, 128), block)
        x = planned(rows, plan, part)
        g = jnp.concatenate([go[part, :], gt[part, :]], axis=1)
        u = jnp.concatenate([uo[part, :], ut[part, :]], axis=1)
        gated[...] += jnp.dot(x, g, preferred_element_type=jnp.float32)
        upward[...] += jnp.dot(x, u, preferred_element_type=jnp.float32)
        return 0

    gated[...] = jnp.zeros_like(gated)
    upward[...] = jnp.zeros_like(upward)
    lax.fori_loop(0, steps, step, 0, unroll=True)
    out[...] = (jax.nn.silu(gated[...]) * upward[...]).astype(jnp.bfloat16)


def hidden_rows(rows, plan, weights):
    width, lanes = weights[0].shape
    count = sum(n for _, _, n in plan)
    whole = pl.BlockSpec(memory_space=pltpu.VMEM)
    return pl.pallas_call(
        functools.partial(hidden_kernel, 7, plan),
        in_specs=[whole] * (len(rows) + 4),
        out_specs=whole,
        out_shape=jax.ShapeDtypeStruct((count, 2 * lanes), jnp.bfloat16),
        scratch_shapes=[pltpu.VMEM((count, 2 * lanes), jnp.float32)] * 2,
        compiler_params=pltpu.CompilerParams(vmem_limit_bytes=VMEM_LIMIT),
        cost_estimate=pl.CostEstimate(
            flops=8 * count * width * lanes,
            bytes_accessed=2 * width * (count + 4 * lanes),
            transcendentals=count * 2 * lanes,
        ),
        name="hidden",
    )(*rows, *weights)


def out_kernel(steps, plan, x_ref, *refs):
    rows, hidden, down, outs, h = refs[:-11], refs[-11:-7], refs[-7:-5], refs[-5:-1], refs[-1]
    pair = outs[0].shape[0]
    lanes = hidden[0].shape[1] // 2
    columns = down[0].shape[1]
    width = RING * columns
    block = columns // steps
    for at, o in enumerate(OFFSETS):
        for core in range(CORES):
            for index, (s, source) in enumerate(zip(OFFSETS, hidden)):
                place = PLACE[(o - s) % RING]
                h[
                    at * pair : (at + 1) * pair,
                    (core * RING + index) * lanes : (core * RING + index + 1) * lanes,
                ] = source[place * pair : (place + 1) * pair, core * lanes : (core + 1) * lanes]
    terms = planned(rows, plan, slice(width, None)).astype(jnp.float32)
    share = terms[:, 0:1] + terms[:, 1:2] + terms[:, 2:3]

    def step(j, _):
        part = pl.ds(pl.multiple_of(j * block, 128), block)
        there = pl.ds(pl.multiple_of(x_ref[0] * columns + j * block, 128), block)
        d = jnp.concatenate([r[:, part] for r in down], axis=0)
        branch = jnp.dot(h[...], d, preferred_element_type=jnp.float32)
        states = planned(rows, plan, there).astype(jnp.float32)
        result = (states + share * branch).astype(jnp.bfloat16)
        for at, out in enumerate(outs):
            out[:, part] = result[at * pair : (at + 1) * pair]
        return 0

    lax.fori_loop(0, steps, step, 0, unroll=True)


def out_rows(x, rows, plan, hidden, down):
    wide = rows[0].shape[1]
    count = sum(n for _, _, n in plan)
    pair = count // RING
    columns = (wide - 128) // RING
    lanes = hidden[0].shape[1]
    whole = pl.BlockSpec(memory_space=pltpu.VMEM)
    return pl.pallas_call(
        functools.partial(out_kernel, 7, plan),
        in_specs=[pl.BlockSpec(memory_space=pltpu.SMEM)] + [whole] * (len(rows) + 6),
        out_specs=[whole] * 4,
        out_shape=[jax.ShapeDtypeStruct((pair, columns), jnp.bfloat16)] * 4,
        scratch_shapes=[pltpu.VMEM((count, RING * lanes), jnp.bfloat16)],
        compiler_params=pltpu.CompilerParams(vmem_limit_bytes=VMEM_LIMIT),
        cost_estimate=pl.CostEstimate(
            flops=2 * count * columns * 4 * lanes,
            bytes_accessed=2 * columns * (2 * count + 4 * lanes),
            transcendentals=0,
        ),
        name="out",
    )(x, *rows, *hidden, *down)


def stack_kernel(*refs):
    depth = refs[0].shape[0]
    for at, piece in enumerate(refs[:-1]):
        refs[-1][at * depth : (at + 1) * depth, :] = piece[...]


def stack(pieces):
    depth, columns = pieces[0].shape
    block = columns // 2
    return pl.pallas_call(
        stack_kernel,
        grid=(2,),
        in_specs=[pl.BlockSpec((depth, block), lambda j: (0, j))] * 4,
        out_specs=pl.BlockSpec((4 * depth, block), lambda j: (0, j)),
        out_shape=jax.ShapeDtypeStruct((4 * depth, columns), jnp.bfloat16),
        compiler_params=pltpu.CompilerParams(vmem_limit_bytes=VMEM_LIMIT),
        name="stack",
    )(*pieces)


def pairs_kernel(a, b, c, d, ab, cd):
    half = a.shape[0]
    ab[:half], ab[half:] = a[...], b[...]
    cd[:half], cd[half:] = c[...], d[...]


def pairs(*arrays):
    half, wide = arrays[0].shape
    whole = pl.BlockSpec(memory_space=pltpu.VMEM)
    return pl.pallas_call(
        pairs_kernel,
        in_specs=[whole] * 4,
        out_specs=[whole] * 2,
        out_shape=[jax.ShapeDtypeStruct((2 * half, wide), arrays[0].dtype)] * 2,
        compiler_params=pltpu.CompilerParams(vmem_limit_bytes=VMEM_LIMIT),
        name="pairs",
    )(*arrays)


def regroup_kernel(x_ref, *refs):
    tails, pieces, outs = refs[:-6], refs[-6:-2], refs[-2:]
    tails = jnp.concatenate([tail[...] for tail in tails], axis=0)
    pair, columns = pieces[0].shape
    capacity = pair // 2
    for direction, out in enumerate(outs):
        part = slice(direction * capacity, (direction + 1) * capacity)
        for offset, piece in zip(OFFSETS, pieces):
            start = pl.multiple_of(lax.rem(x_ref[0] - offset + RING, RING) * columns, 128)
            out[:, pl.ds(start, columns)] = piece[part, :]
        out[:, RING * columns :] = tails[part]


def regroup(x, rows, pieces):
    pair, columns = pieces[0].shape
    wide = RING * columns + 128
    whole = pl.BlockSpec((pair, columns), lambda j, x: (0, 0))
    return pl.pallas_call(
        regroup_kernel,
        grid_spec=pltpu.PrefetchScalarGridSpec(
            num_scalar_prefetch=1,
            grid=(1,),
            in_specs=[
                pl.BlockSpec((r.shape[0], 128), lambda j, x: (0, RING * columns // 128))
                for r in rows
            ]
            + [whole] * 4,
            out_specs=[pl.BlockSpec((pair // 2, wide), lambda j, x: (0, 0))] * 2,
        ),
        out_shape=[jax.ShapeDtypeStruct((pair // 2, wide), jnp.bfloat16)] * 2,
        compiler_params=pltpu.CompilerParams(vmem_limit_bytes=VMEM_LIMIT),
        name="regroup",
    )(x, *rows, *pieces)


def merge_kernel(*refs):
    pieces, outs = refs[:-2], refs[-2:]
    count, width = outs[0].shape
    token = lax.broadcasted_iota(jnp.int32, (count, count), 1).astype(jnp.float32)
    for direction, out in enumerate(outs):
        mine = pieces[direction::2]
        rows = jnp.concatenate([piece[:, :width] for piece in mine], axis=0)
        place = jnp.concatenate([piece[:, width:] for piece in mine], axis=0).astype(jnp.float32)
        pick = jnp.where(place[:, 3:4] == token, 1.0, 0.0).astype(jnp.bfloat16)
        out[...] = lax.dot_general(
            pick, rows, (((0,), (0,)), ((), ())), preferred_element_type=jnp.float32
        ).astype(jnp.bfloat16)


def merge(pieces):
    count = sum(piece.shape[0] for piece in pieces) // 2
    whole = pl.BlockSpec(memory_space=pltpu.VMEM)
    shape = jax.ShapeDtypeStruct((count, pieces[0].shape[1] - 128), jnp.bfloat16)
    return pl.pallas_call(
        merge_kernel,
        in_specs=[whole] * len(pieces),
        out_specs=[whole] * 2,
        out_shape=[shape] * 2,
        compiler_params=pltpu.CompilerParams(vmem_limit_bytes=VMEM_LIMIT),
        name="merge",
    )(*pieces)


def after(values, deps):
    return lax.optimization_barrier((tuple(values), tuple(deps)))[0]


def per_device(
    forward_states,
    reverse_states,
    forward_routes,
    reverse_routes,
    forward_share,
    reverse_share,
    layer_gate,
    layer_up,
    layer_down,
):
    pipes = lax.axis_size("pipe")
    send = functools.partial(move, pipes=pipes)
    mine = lax.axis_index("ep").astype(jnp.int32)
    z = mine // (RING * CORES)
    x = (mine // CORES) % RING
    count, width = forward_states.shape[1:]
    columns = width // RING
    gate, up, down = layer_gate[0], layer_up[0], layer_down[0]

    at_x = x[None]

    def spread(h):
        return [h] + [send(h, steps=-o) for o in OFFSETS[1:]]

    def back(outs):
        return [outs[0]] + [send(out, steps=o) for out, o in zip(outs[1:], OFFSETS[1:])]

    def first(f, r):
        return send(f, steps=1), send(r, steps=-1)

    with jax.named_scope("weights"):
        weights = [gate, send(gate, core=True), up, send(up, core=True)]

    with jax.named_scope("pack"):
        own_f, own_r, oth = pack(
            jnp.stack([mine, z]),
            forward_routes.reshape(1, -1),
            reverse_routes.reshape(1, -1),
            forward_share.reshape(1, count),
            reverse_share.reshape(1, count),
            forward_states[0],
            reverse_states[0],
        )
    half = count // 2
    with jax.named_scope("swap"):
        swapped = send(oth, flip=True)
    with jax.named_scope("first1"):
        own_left_f, own_right_r = first(own_f, own_r)

    with jax.named_scope("down"):
        parts = list(slices(after((at_x,), (own_f,))[0], down))
        parts[1:3] = after(parts[1:3], (weights[1], weights[3]))
        parts[1:3] = [send(part, steps=-o) for part, o in zip(parts[1:3], OFFSETS[1:3])]

        parts[3:] = after(parts[3:], (own_left_f, own_right_r))
        parts[3] = send(parts[3], steps=-OFFSETS[3])
    plan = (
        *((0, 0, half), (1, 0, half)),
        *((2, 0, half), (4, half, half)),
        *((5, half, half), (3, 0, half)),
        *((4, 0, half), (5, 0, half)),
    )

    def gather(f, r, left_f, right_r, dep):
        left_f, right_r = after((left_f, right_r), dep)
        onward, backward = pairs(left_f, r, right_r, f)
        onward, backward = send(onward, steps=1), send(backward, steps=-1)
        return [f, r, left_f, right_r, onward, backward]

    with jax.named_scope("second1"):
        rows1 = gather(own_f, own_r, own_left_f, own_right_r, parts[1:3])
    with jax.named_scope("down"):
        half_down = stack(parts)
        down = [half_down, send(half_down, core=True)]
    with jax.named_scope("first0"):
        (swapped,) = after((swapped,), parts[1:])
        f, r = swapped[:half], swapped[half:]
        left_f, right_r = first(f, r)
    with jax.named_scope("hidden1"):
        hidden1 = spread(hidden_rows(after(rows1, down[1:]), plan, weights))
    with jax.named_scope("second0"):
        rows0 = gather(f, r, left_f, right_r, hidden1[1:])
    with jax.named_scope("out1"):
        outs1 = out_rows(at_x, rows1, plan, hidden1, down)
    with jax.named_scope("back1"):
        back1 = back(outs1)
    with jax.named_scope("hidden0"):
        hidden0 = spread(hidden_rows(rows0, plan, weights))
    with jax.named_scope("relay1"):
        whole_f, whole_r = regroup(at_x, [own_f, own_r], after(back1, hidden0[1:]))
        sent1 = [send(whole_f, by=1), send(whole_r, by=-1)]
    with jax.named_scope("out0"):
        outs0 = out_rows(at_x, rows0, plan, hidden0, down)
    with jax.named_scope("back0"):
        back0 = back(outs0)
    with jax.named_scope("relay0"):
        whole_f, whole_r = regroup(at_x, [swapped], back0)
        sent0 = [send(whole_f, by=1, flip=True), send(whole_r, by=-1, flip=True)]
    with jax.named_scope("merge"):
        ahead, behind = merge(sent1 + sent0)
    return (ahead[None], behind[None])


def solution(mesh):
    in_specs = (
        P("pipe", "ep", None),
        P("pipe", "ep", None),
        P(None, "pipe", None, None),
        P(None, "pipe", None, None),
        P(None, "pipe", "ep"),
        P(None, "pipe", "ep"),
        P("pipe", None, "ep"),
        P("pipe", None, "ep"),
        P("pipe", "ep", None),
    )
    out_specs = (P("pipe", "ep", None), P("pipe", "ep", None))
    return jax.shard_map(
        per_device, mesh=mesh, in_specs=in_specs, out_specs=out_specs, check_vma=False
    )
```
